128 devices in a mesh: exp: 16 (over z_lo, y, core), fsdp: 8 (over z_hi, x).
Axes of the slice: x: 4, y: 4, z: 4 (z_hi: 2, z_lo: 2; z = z_hi * 2 + z_lo), core: 2. Of those that a mesh axis runs over, the one named last changes fastest.
Arguments:
- tokens: bfloat16 [512, 7168], P(('exp', 'fsdp')), may hold values from -6 to 6
- expert_ids: int32 [512, 8], P(('exp', 'fsdp')), may hold values from 0 to 31, all different within a row; in each aligned block of 4 rows (0 to 3, 4 to 7, ...) at most 2 rows name the same one
- combine_weight: float32 [512, 8], P(('exp', 'fsdp')), may hold values from 0.1 to 1
- gate_weight: bfloat16 [32, 7168, 2048], P('exp', 'fsdp'), may hold values from -0.0625 to 0.0625
- up_weight: bfloat16 [32, 7168, 2048], P('exp', 'fsdp'), may hold values from -0.0625 to 0.0625
- down_weight: bfloat16 [32, 7168, 2048], P('exp', 'fsdp'), may hold values from -0.125 to 0.125
Outputs:
- mixed: bfloat16 [512, 7168], P(('exp', 'fsdp'))
The draws below stay inside these ranges and needn't reach their ends.
Inputs may be any that keep to these rules, and one draw needn't show every extreme that they name: `expert_ids`: each row names 8 different experts. Among the 4 rows of one device no expert is named more than 2 times, a bound that some block reaches.
All inputs are finite; a program needn't handle non-finite values.
Results may differ from the reference program's by a relative error of at most 0.025.
Values may be sent and summed in bfloat16 or wider, within the bound.
No kernel may reach another device: no remote copies, remote signals or barrier semaphores. Data moves between devices by JAX's collectives and lax.ppermute only.
A program may use at most 192 MiB of HBM per device.

```python
import math
import jax
import jax.numpy as jnp
import numpy as np
from jax import lax

D = 7168
FF = 2048
TOP = 8
ROWS_DEV = 4
EXPERTS = 32
TOKENS = 512
CAP = 2
SLICE = 256
N_FSDP = 8


def levels(own_key, dims, pieces, low, top_value):
    gain, own = 1.0, jax.random.fold_in(own_key, 6)
    for position, blocks in pieces:
        draws = jnp.exp(jax.random.uniform(jax.random.fold_in(own, position), (blocks,), jnp.float32, low / len(pieces), top_value / len(pieces)))
        gain = gain * jnp.repeat(draws, dims[position] // blocks).reshape([-1 if axis == position else 1 for axis in range(len(dims))])
    return gain


def assign_block(rng, own, number, rows, amount, top, bound, lean):
    sequence = jax.random.permutation(rng, amount)
    heavy_load, common = shares(amount, rows * top, bound, lean, True), shares(amount, rows * top, bound, lean, False)
    places = jnp.arange(amount)

    def named(lengths, offset_by):
        used = int((lengths > 0).sum())
        fixed = max(1, used // 4)
        passed = fixed + (places - fixed + offset_by * (used - fixed)) % max(1, amount - fixed)
        return jnp.zeros((amount,), jnp.int32).at[sequence[jnp.where(places < fixed, places, passed)]].set(jnp.asarray(lengths, jnp.int32))

    lengths = jnp.where(number % 4 == 0, named(heavy_load, number // 4), named(common, number - number // 4 - 1))
    mixed = jax.random.permutation(jax.random.fold_in(own, 3), amount)
    giver, receiver = mixed[0:amount // 2 * 2:2], mixed[1:amount // 2 * 2:2]
    slack = jnp.minimum(lengths[giver] - 1, bound - lengths[receiver]) // 2
    slack = jnp.where((giver == sequence[0]) | (receiver == sequence[0]) | (lengths[receiver] == 0), 0, jnp.maximum(slack, 0))
    passed = jax.random.randint(jax.random.fold_in(own, 4), (amount // 2,), 0, 1 << 20) % (slack + 1)
    lengths = lengths.at[giver].add(-passed).at[receiver].add(passed)
    members = jnp.searchsorted(jnp.cumsum(lengths), jnp.arange(rows * top), side="right").astype(jnp.int32)
    grid = members.reshape(top, rows).T
    grid = grid[jax.random.permutation(jax.random.fold_in(own, 1), rows)]
    offset_by = jax.random.randint(jax.random.fold_in(own, 2), (rows, 1), 0, top)
    return jnp.take_along_axis(grid, (jnp.arange(top)[None, :] + offset_by) % top, axis=1)


def shares(amount, total, limit, lean, full):
    loads = [(1 << 20) // math.isqrt(rank ** lean) + 1 for rank in range(1, amount + 1)]
    largest = limit if full else min(limit, max(-(-total // amount), total * loads[0] // sum(loads)))
    least = 1 if total - largest >= amount - 1 else 0
    given, spare = [largest] + [least] * (amount - 1), total - largest - least * (amount - 1)
    while spare > 0:
        candidates = [i for i in range(1, amount) if given[i] < largest] or [i for i in range(1, amount) if given[i] < limit]
        mass, left = sum([loads[i] for i in candidates]), spare
        for i in candidates:
            more = min(limit - given[i], max(1, left * loads[i] // mass), spare)
            given[i] = given[i] + more
            spare = spare - more
    return np.array(given)


def centred(rng, dims, deviation, reach, cuts=(), kind=jnp.bfloat16):
    loudness = levels(rng, dims, cuts, -0.22, 0.18) if cuts else 1.0
    drawn = jax.random.normal(rng, dims, jnp.float32) * deviation * loudness
    return jnp.minimum(jnp.maximum(drawn, -reach), reach).astype(kind)


def setup_inputs(seed: int = 0) -> dict:
    streams_of = jax.random.split(jax.random.key(seed), 7)
    tokens = centred(streams_of[0], (TOKENS, D), 1.0, 6.0, ((0, 128),))
    expert_ids_keys = jax.random.split(jax.random.fold_in(streams_of[1], 1), TOKENS // ROWS_DEV)
    expert_ids_turns = jax.random.permutation(jax.random.fold_in(streams_of[1], 3), TOKENS // ROWS_DEV)
    expert_ids = jax.vmap(lambda own, number: assign_block(jax.random.fold_in(streams_of[1], 2), own, number, ROWS_DEV, EXPERTS, TOP, CAP, 2))(expert_ids_keys, expert_ids_turns).reshape((TOKENS, TOP))
    combine_weight = jnp.clip(jnp.exp(math.log(1.0) - 2.3025851 * jax.random.uniform(streams_of[2], (TOKENS, TOP), jnp.float32) ** levels(streams_of[2], (TOKENS, TOP), ((0, 128),), -0.2, 0.2)), 0.1, 1.0)
    gate_weight = centred(streams_of[3], (EXPERTS, D, FF), D ** -0.5, 0.0625, ((0, 16), (1, 8)))
    up_weight = centred(streams_of[4], (EXPERTS, D, FF), D ** -0.5, 0.0625, ((0, 16), (1, 8)))
    down_weight = centred(streams_of[5], (EXPERTS, D, FF), FF ** -0.5, 0.125, ((0, 16), (1, 8)))
    return {"tokens": tokens, "expert_ids": expert_ids, "combine_weight": combine_weight, "gate_weight": gate_weight, "up_weight": up_weight, "down_weight": down_weight}


ROUTE_SCALE = 2.827


def reference(tokens, expert_ids, combine_weight, gate_weight, up_weight, down_weight):
    route_gate = ROUTE_SCALE * combine_weight / jnp.sum(combine_weight, axis=1, keepdims=True)
    expert_iota = jnp.arange(EXPERTS, dtype=jnp.int32)
    chosen = (expert_ids[:, :, None] == expert_iota[None, None, :]).astype(jnp.float32)
    route_coef = jnp.sum(route_gate[:, :, None] * chosen, axis=1)

    def one_expert(running_sum, expert_inputs):
        gate_matrix, up_matrix, down_matrix, coef_column = expert_inputs
        gate_proj = jnp.dot(tokens, gate_matrix, preferred_element_type=jnp.float32)
        up_proj = jnp.dot(tokens, up_matrix, preferred_element_type=jnp.float32)
        hidden = (jax.nn.silu(gate_proj) * up_proj).astype(jnp.bfloat16)
        row_count = hidden.shape[0]
        hidden_blocks = hidden.reshape(row_count, N_FSDP, SLICE).astype(jnp.float32)
        down_blocks = down_matrix.reshape(D, N_FSDP, SLICE).astype(jnp.float32)
        slice_partial = jnp.einsum("nsf,dsf->nsd", hidden_blocks, down_blocks).astype(jnp.bfloat16)
        expert_out = jnp.sum(slice_partial.astype(jnp.float32), axis=1).astype(jnp.bfloat16)
        return running_sum + coef_column[:, None] * expert_out.astype(jnp.float32), None

    start_sum = jnp.zeros((TOKENS, D), jnp.float32)
    running_sum, _ = lax.scan(one_expert, start_sum, (gate_weight, up_weight, down_weight, route_coef.T))
    return running_sum.astype(jnp.bfloat16)
```

```python
import jax
import jax.numpy as jnp
from jax import lax
from jax.experimental import pallas as pl
from jax.experimental.pallas import tpu as pltpu
from jax.sharding import PartitionSpec as P

ROUTE_SCALE = 2.827
META = 128
BOTH = ("exp", "fsdp")


def params(mib):
    return pltpu.CompilerParams(vmem_limit_bytes=mib * 1024 * 1024)


def dot(a, b, dims):
    return lax.dot_general(a, b, (dims, ((), ())), preferred_element_type=jnp.float32)


def pack_rows(tokens, expert_ids, combine_weight, exp_count, fsdp_count, local_experts):
    rows, width = tokens.shape
    experts = exp_count * local_experts
    picked = expert_ids[:, :, None] == jnp.arange(experts, dtype=jnp.int32)[None, None, :]
    route_gate = ROUTE_SCALE * combine_weight / jnp.sum(combine_weight, axis=1, keepdims=True)
    share = jnp.sum(jnp.where(picked, route_gate[:, :, None], 0.0), axis=1)
    hits = jnp.any(picked, axis=1).astype(jnp.int32)
    earlier = jnp.stack([jnp.sum(hits[:row], axis=0) for row in range(rows)])
    code = (hits * (earlier + 1)).astype(jnp.bfloat16)
    high = share.astype(jnp.bfloat16)
    low = (share - high.astype(jnp.float32)).astype(jnp.bfloat16)
    meta = jnp.stack([code, high, low], axis=1).reshape(rows, 3, exp_count, local_experts)
    meta = meta.transpose(2, 0, 1, 3).reshape(exp_count, 1, rows, 3 * local_experts)
    meta = jnp.pad(meta, ((0, 0), (0, 0), (0, 0), (0, META - 3 * local_experts)))
    slices = tokens.reshape(rows, fsdp_count, width // fsdp_count).transpose(1, 0, 2)[None]
    return jnp.concatenate(
        [
            jnp.broadcast_to(slices, (exp_count,) + slices.shape[1:]),
            jnp.broadcast_to(meta, (exp_count, fsdp_count) + meta.shape[2:]),
        ],
        axis=3,
    )


def placing(meta, local, slots, rows_dev):
    rows = meta.shape[0]
    code = meta[:, local : local + 1].astype(jnp.float32).astype(jnp.int32)
    cap = slots * rows_dev // rows
    block = lax.broadcasted_iota(jnp.int32, (rows, 1), 0) // rows_dev
    slot = jnp.where(code > 0, block * cap + code - 1, -1)
    return (slot == lax.broadcasted_iota(jnp.int32, (rows, slots), 1)).astype(jnp.bfloat16)


def project(rows_in, gate_weight, up_weight, slots, rows_dev, fsdp_count, tile):
    experts, depth, units = gate_weight.shape
    rows = rows_in.shape[0]
    part = slots // fsdp_count

    def body(rows_ref, gate_ref, up_ref, out_ref, held):
        local = pl.program_id(0)

        @pl.when(pl.program_id(1) == 0)
        def _():
            meta = rows_ref[:, depth:]
            for index in range(experts):

                @pl.when(local == index)
                def _():
                    place = placing(meta, index, slots, rows_dev)
                    held[...] = dot(place, rows_ref[:, :depth], ((0,), (0,))).astype(jnp.bfloat16)

        for which, ref in enumerate((gate_ref, up_ref)):
            value = dot(held[...], ref[0], ((1,), (0,))).astype(jnp.bfloat16)
            out_ref[:, 0, which] = value.reshape(fsdp_count, part, tile)

    return pl.pallas_call(
        body,
        grid=(experts, units // tile),
        out_shape=jax.ShapeDtypeStruct((fsdp_count, experts, 2, part, units), jnp.bfloat16),
        in_specs=[
            pl.BlockSpec((rows, rows_in.shape[1]), lambda e, n: (0, 0)),
            pl.BlockSpec((1, depth, tile), lambda e, n: (e, 0, n)),
            pl.BlockSpec((1, depth, tile), lambda e, n: (e, 0, n)),
        ],
        out_specs=pl.BlockSpec((fsdp_count, 1, 2, part, tile), lambda e, n: (0, e, 0, 0, n)),
        scratch_shapes=[pltpu.VMEM((slots, depth), jnp.bfloat16)],
        compiler_params=params(40),
        cost_estimate=pl.CostEstimate(
            flops=4 * experts * slots * depth * units,
            bytes_accessed=4 * experts * depth * units + 4 * experts * slots * units,
            transcendentals=0,
        ),
    )(rows_in, gate_weight, up_weight)


def activate(partials, tile):
    fsdp_count, experts, _, part, units = partials.shape

    def body(in_ref, out_ref):
        total = in_ref[0].astype(jnp.float32)
        for source in range(1, fsdp_count):
            total += in_ref[source].astype(jnp.float32)
        gate, up = total[:, 0], total[:, 1]
        hidden = (gate / (1.0 + jnp.exp(-gate)) * up).astype(jnp.bfloat16)
        for target in range(fsdp_count):
            out_ref[target] = hidden

    return pl.pallas_call(
        body,
        grid=(units // tile,),
        out_shape=jax.ShapeDtypeStruct((fsdp_count, experts, part, units), jnp.bfloat16),
        in_specs=[pl.BlockSpec((fsdp_count, experts, 2, part, tile), lambda n: (0, 0, 0, 0, n))],
        out_specs=pl.BlockSpec((fsdp_count, experts, part, tile), lambda n: (0, 0, 0, n)),
        compiler_params=params(40),
    )(partials)


def finish(rows_in, hidden, down_weight, slots, rows_dev, tile):
    fsdp_count, experts, part, units = hidden.shape
    features = down_weight.shape[1]
    rows = rows_in.shape[0]
    steps = units // tile

    def body(meta_ref, hidden_ref, down_ref, out_ref, total, mixed):
        local, step = pl.program_id(0), pl.program_id(1)
        value = dot(hidden_ref[:, 0].reshape(slots, tile), down_ref[0], ((1,), (1,)))

        @pl.when(step == 0)
        def _():
            total[...] = value

        @pl.when(step > 0)
        def _():
            total[...] += value

        for index in range(experts):

            @pl.when((local == index) & (step == steps - 1))
            def _():
                meta = meta_ref[...]
                place = placing(meta, index, slots, rows_dev)
                high = meta[:, experts + index : experts + index + 1].astype(jnp.float32)
                low = meta[:, 2 * experts + index : 2 * experts + index + 1].astype(jnp.float32)
                term = dot(place, total[...].astype(jnp.bfloat16), ((1,), (0,))) * (high + low)
                if index == 0:
                    mixed[...] = term
                else:
                    mixed[...] += term
                if index == experts - 1:
                    out_ref[...] = mixed[...].astype(jnp.bfloat16)

    return pl.pallas_call(
        body,
        grid=(experts, steps),
        out_shape=jax.ShapeDtypeStruct((rows, features), jnp.bfloat16),
        in_specs=[
            pl.BlockSpec((rows, META), lambda e, k: (0, features // META)),
            pl.BlockSpec((fsdp_count, 1, part, tile), lambda e, k: (0, e, 0, k)),
            pl.BlockSpec((1, features, tile), lambda e, k: (e, 0, k)),
        ],
        out_specs=pl.BlockSpec((rows, features), lambda e, k: (0, 0)),
        scratch_shapes=[pltpu.VMEM((slots, features), jnp.float32), pltpu.VMEM((rows, features), jnp.float32)],
        compiler_params=params(40),
        cost_estimate=pl.CostEstimate(
            flops=2 * experts * slots * features * units,
            bytes_accessed=2 * experts * features * units + 2 * experts * slots * units,
            transcendentals=0,
        ),
    )(rows_in, hidden, down_weight)


def on_device(tokens, expert_ids, combine_weight, gate_weight, up_weight, down_weight):
    exp_count, fsdp_count = lax.axis_size("exp"), lax.axis_size("fsdp")
    devices = exp_count * fsdp_count
    rows_dev, width = tokens.shape
    local_experts, depth, units = gate_weight.shape
    experts = exp_count * local_experts
    cap = max(2, rows_dev * expert_ids.shape[1] * 3 // (2 * experts))
    slots = devices * cap
    sent = pack_rows(tokens, expert_ids, combine_weight, exp_count, fsdp_count, local_experts)
    sent = sent.reshape((devices,) + sent.shape[2:])
    rows_in = lax.all_to_all(sent, BOTH, 0, 0, tiled=True).reshape(devices * rows_dev, depth + META)
    partials = project(rows_in, gate_weight, up_weight, slots, rows_dev, fsdp_count, 512)
    partials = lax.all_to_all(partials, "fsdp", 0, 0, tiled=True)
    hidden = activate(partials, 256)
    hidden = lax.all_to_all(hidden, "fsdp", 0, 0, tiled=True)
    mixed = finish(rows_in, hidden, down_weight, slots, rows_dev, 512)
    home = lax.all_to_all(mixed.reshape(devices, rows_dev, depth), BOTH, 0, 0, tiled=True)
    home = home.reshape(exp_count, fsdp_count, rows_dev, depth).astype(jnp.float32)
    return jnp.sum(home, axis=0).astype(jnp.bfloat16).transpose(1, 0, 2).reshape(rows_dev, width)


def solution(mesh):
    return jax.shard_map(
        on_device,
        mesh=mesh,
        in_specs=(
            P(BOTH, None),
            P(BOTH, None),
            P(BOTH, None),
            P("exp", "fsdp", None),
            P("exp", "fsdp", None),
            P("exp", "fsdp", None),
        ),
        out_specs=P(BOTH, None),
        check_vma=False,
    )
```

```python
import jax
import jax.numpy as jnp
from jax import lax
from jax.experimental import pallas as pl
from jax.experimental.pallas import tpu as pltpu
from jax.sharding import PartitionSpec as P

ROUTE_SCALE = 2.827
META = 128
UNIT = 128
RING = 4
BOTH = ("exp", "fsdp")


def params(mib):
    return pltpu.CompilerParams(vmem_limit_bytes=mib * 1024 * 1024)


def dot(a, b, dims):
    return lax.dot_general(a, b, (dims, ((), ())), preferred_element_type=jnp.float32)


def pack_rows(tokens, expert_ids, combine_weight, exp_count, fsdp_count, experts):
    rows, width = tokens.shape
    depth = width // fsdp_count

    def body(tokens_ref, ids_ref, weight_ref, out_ref):
        ids, weight = ids_ref[...], weight_ref[...]
        gates = ROUTE_SCALE * weight / jnp.sum(weight, axis=1, keepdims=True)
        column = lax.broadcasted_iota(jnp.int32, (rows, META), 1)
        hits = jnp.zeros((rows, META), jnp.float32)
        high_low = jnp.zeros((rows, META), jnp.float32)
        for k in range(ids.shape[1]):
            named, gate = ids[:, k : k + 1], gates[:, k : k + 1]
            high = gate.astype(jnp.bfloat16).astype(jnp.float32)
            hits = jnp.where(column == named, 1.0, hits)
            high_low = jnp.where(column == named + experts, high, high_low)
            high_low = jnp.where(column == named + 2 * experts, gate - high, high_low)
        meta = jnp.where(column < experts, hits, high_low).astype(jnp.bfloat16)
        for f in range(fsdp_count):
            block = jnp.concatenate([tokens_ref[:, f * depth : (f + 1) * depth], meta], axis=1)
            for e in range(exp_count):
                out_ref[e, f] = block

    return pl.pallas_call(
        body,
        out_shape=jax.ShapeDtypeStruct((exp_count, fsdp_count, rows, depth + META), jnp.bfloat16),
        compiler_params=params(32),
    )(tokens, expert_ids, combine_weight)


def position(target, me):
    across = (target // RING + me // RING) % 2
    along = (target + 2 * RING - me) % RING
    return jnp.where(along < 2, along, 5 - along) * 2 + across


def gather_rows(me, rows_in, experts, total, slots):
    rows, depth = rows_in.shape[0], rows_in.shape[1] - META
    part = UNIT // (2 * RING)

    def body(me_ref, rows_ref, out_ref, info_ref, full_ref):
        meta = rows_ref[:, depth:]
        before = lax.broadcasted_iota(jnp.int32, (rows, rows), 1) < lax.broadcasted_iota(jnp.int32, (rows, rows), 0)
        source = lax.broadcasted_iota(jnp.int32, (META, META), 0)
        target = lax.broadcasted_iota(jnp.int32, (META, META), 1)
        wanted = target // experts * total + me_ref[1] * experts + target % experts
        chosen = ((source == wanted) & (target < 3 * experts)).astype(jnp.bfloat16)
        meta = dot(meta, chosen, ((1,), (0,)))
        rank = dot(before.astype(jnp.bfloat16), meta.astype(jnp.bfloat16), ((1,), (0,)))
        column = lax.broadcasted_iota(jnp.int32, (rows, META), 1)
        info = jnp.zeros((rows, META), jnp.float32)
        for index in range(experts):
            hit = meta[:, index : index + 1]
            slot = jnp.where(hit > 0.5, rank[:, index : index + 1], -1.0)
            gate = meta[:, experts + index : experts + index + 1] + meta[:, 2 * experts + index : 2 * experts + index + 1]
            info = jnp.where(column == index, slot, jnp.where(column == experts + index, gate, info))
            place = slot.astype(jnp.int32) == lax.broadcasted_iota(jnp.int32, (rows, slots), 1)
            value = dot(place.astype(jnp.bfloat16), rows_ref[:, :depth], ((0,), (0,))).astype(jnp.bfloat16)
            for block in range(slots // part):
                first = block * part // UNIT * UNIT + position(block % (2 * RING), me_ref[0]) * part
                out_ref[index, pl.ds(pl.multiple_of(first, part), part)] = value[block * part : (block + 1) * part]
            full_ref[index] = (jnp.sum(hit) > UNIT).astype(jnp.int32)
        info_ref[...] = info

    return pl.pallas_call(
        body,
        out_shape=(
            jax.ShapeDtypeStruct((experts, slots, depth), jnp.bfloat16),
            jax.ShapeDtypeStruct((rows, META), jnp.float32),
            jax.ShapeDtypeStruct((experts,), jnp.int32),
        ),
        out_specs=(
            pl.BlockSpec(memory_space=pltpu.VMEM),
            pl.BlockSpec(memory_space=pltpu.VMEM),
            pl.BlockSpec(memory_space=pltpu.SMEM),
        ),
        in_specs=[pl.BlockSpec(memory_space=pltpu.SMEM), pl.BlockSpec(memory_space=pltpu.VMEM)],
        compiler_params=params(32),
    )(me, rows_in)


def extra_unit(units, experts, local):
    return experts + local if units == 2 * experts else experts


def project(full, packed, weight, units, z_first, tile):
    experts, depth, width = weight.shape
    slots = packed.shape[1]
    part = UNIT // (2 * RING)

    def body(full_ref, packed_ref, weight_ref, *outs):
        column = pl.ds(pl.multiple_of(pl.program_id(0) * tile, tile), tile)
        local = pl.program_id(1)

        def put(unit, value):
            value = value.reshape(2 * RING, part, tile)
            for order in range(RING):
                if z_first:
                    sent, kept = outs
                    kept[order, unit, :, column] = value[2 * order]
                    sent[order, unit, :, column] = value[2 * order + 1]
                else:
                    outs[order][:, unit, :, column] = value[2 * order : 2 * order + 2]

        @pl.when(full_ref[local] == 0)
        def _():
            put(local, dot(packed_ref[local, :UNIT], weight_ref[0], ((1,), (0,))).astype(jnp.bfloat16))

        if units > experts:

            @pl.when(full_ref[local] != 0)
            def _():
                value = dot(packed_ref[local], weight_ref[0], ((1,), (0,))).astype(jnp.bfloat16)
                put(local, value[:UNIT])
                put(extra_unit(units, experts, local), value[UNIT:])

    shapes = [(RING, units, part, width)] * 2 if z_first else [(2, units, part, width)] * RING
    return pl.pallas_call(
        body,
        grid=(width // tile, experts),
        out_shape=tuple(jax.ShapeDtypeStruct(shape, jnp.bfloat16) for shape in shapes),
        in_specs=[
            pl.BlockSpec(memory_space=pltpu.SMEM),
            pl.BlockSpec(memory_space=pltpu.VMEM),
            pl.BlockSpec((1, depth, tile), lambda n, e: (e, 0, n)),
        ],
        out_specs=tuple(pl.BlockSpec(memory_space=pltpu.VMEM) for _ in shapes),
        compiler_params=params(32),
        cost_estimate=pl.CostEstimate(
            flops=2 * units * UNIT * depth * width,
            bytes_accessed=2 * experts * depth * width + 2 * units * UNIT * width,
            transcendentals=0,
        ),
    )(full, packed, weight)


def in_pieces(shape, piece, body):
    units, _, width = shape

    def step(index, carry):
        body(index // (width // piece), pl.ds(pl.multiple_of(index % (width // piece) * piece, piece), piece))
        return carry

    lax.fori_loop(0, units * (width // piece), step, 0)


def whole_call(body, shapes, *operands):
    return pl.pallas_call(
        body,
        out_shape=tuple(jax.ShapeDtypeStruct(shape, kind) for shape, kind in shapes),
        in_specs=[pl.BlockSpec(memory_space=pltpu.VMEM)] * len(operands),
        out_specs=tuple(pl.BlockSpec(memory_space=pltpu.VMEM) for _ in shapes),
        compiler_params=params(32),
    )(*operands)


def wide(value):
    return value.astype(jnp.float32)


def fold(kept, came):
    block = kept.shape[1:]

    def body(kept_ref, came_ref, *outs):
        for order, out_ref in enumerate(outs):

            def piece(unit, column):
                total = wide(kept_ref[order, unit, :, column]) + wide(came_ref[order, unit, :, column])
                out_ref[unit, :, column] = total.astype(jnp.bfloat16)

            in_pieces(block, 512, piece)

    return whole_call(body, [(block, jnp.bfloat16)] * RING, kept, came)


def add_along(*terms):
    block = terms[0].shape[1:]

    def body(*refs):
        for side, out_ref in ((1, refs[-2]), (0, refs[-1])):

            def piece(unit, column):
                total = sum(wide(ref[side, unit, :, column]) for ref in refs[1:-2])
                out_ref[unit, :, column] = (total + wide(refs[0][side, unit, :, column])).astype(out_ref.dtype)

            in_pieces(block, 512, piece)

    return whole_call(body, [(block, jnp.bfloat16), (block, jnp.float32)], *terms)


def activate(stays, came, *terms):
    block = stays.shape

    def body(stays_ref, came_ref, *refs):
        def piece(unit, column):
            gate = stays_ref[unit, :, column] + wide(came_ref[unit, :, column])
            up = sum(wide(ref[unit, :, column]) for ref in refs[1:-1]) + wide(refs[0][unit, :, column])
            refs[-1][unit, :, column] = (gate / (1.0 + jnp.exp(-gate)) * up).astype(jnp.bfloat16)

        in_pieces(block, 512, piece)

    return whole_call(body, [(block, jnp.bfloat16)], stays, came, *terms)[0]


def along(value, step):
    return lax.ppermute(value, "fsdp", [(i, i // RING * RING + (i + step) % RING) for i in range(2 * RING)])


def across(value):
    return lax.ppermute(value, "fsdp", [(i, (i + RING) % (2 * RING)) for i in range(2 * RING)])


def to_others(kept, right, left, far):
    return kept, along(right, 1), along(left, -1), along(far, 2)


def from_others(value):
    return along(value, -1), along(value, 1), along(value, 2)


def finish(full, me, info, parts, down_weight, tile):
    units, part, width = parts[0].shape
    experts, features = down_weight.shape[:2]
    rows = info.shape[0]
    count = len(parts)

    def body(full_ref, me_ref, info_ref, *refs):
        part_refs, (down_ref, out_ref, hidden, total, mixed) = refs[:count], refs[count:]
        local = pl.program_id(0)

        @pl.when(local == 0)
        def _():
            mixed[...] = jnp.zeros_like(mixed)

        def put(slots):
            for index, ref in enumerate(part_refs):
                order, side = index // 2, index % 2
                step = (0, 1, RING - 1, 2)[order]
                target = (me_ref[0] // RING + side) % 2 * RING + (me_ref[0] + step) % RING
                for first in range(0, slots, UNIT):
                    unit = extra_unit(units, experts, local) if first else local
                    hidden[pl.ds(pl.multiple_of(target * part + first, part), part)] = ref[unit]

            def step(index, carry):
                chosen = pl.ds(pl.multiple_of(index * tile, tile), tile)
                value = dot(down_ref[local, chosen], hidden[:slots], ((1,), (1,)))
                total[chosen, :slots] = value.astype(jnp.bfloat16)
                return carry

            lax.fori_loop(0, features // tile, step, 0)
            slot = jnp.where(local == 0, info_ref[:, :1], info_ref[:, 1:2])
            gate = jnp.where(local == 0, info_ref[:, 2:3], info_ref[:, 3:4])
            place = slot.astype(jnp.int32) == lax.broadcasted_iota(jnp.int32, (rows, slots), 1)
            mixed[...] += dot(place.astype(jnp.bfloat16), total[:, :slots], ((1,), (1,))) * gate

        @pl.when(full_ref[local] == 0)
        def _():
            put(UNIT)

        if units > experts:

            @pl.when(full_ref[local] != 0)
            def _():
                put(2 * UNIT)

        @pl.when(local == experts - 1)
        def _():
            out_ref[...] = mixed[...].astype(jnp.bfloat16)

    scalars, whole = pl.BlockSpec(memory_space=pltpu.SMEM), pl.BlockSpec(memory_space=pltpu.VMEM)
    return pl.pallas_call(
        body,
        grid=(experts,),
        out_shape=jax.ShapeDtypeStruct((rows, features), jnp.bfloat16),
        in_specs=[scalars, scalars] + [whole] * (count + 2),
        out_specs=whole,
        scratch_shapes=[
            pltpu.VMEM((2 * UNIT, width), jnp.bfloat16),
            pltpu.VMEM((features, 2 * UNIT), jnp.bfloat16),
            pltpu.VMEM((rows, features), jnp.float32),
        ],
        compiler_params=params(24),
        cost_estimate=pl.CostEstimate(
            flops=2 * units * UNIT * features * width,
            bytes_accessed=2 * experts * features * width + 2 * units * UNIT * width,
            transcendentals=0,
        ),
    )(full, me, info, *parts, down_weight)


def on_device(tokens, expert_ids, combine_weight, gate_weight, up_weight, down_weight):
    exp_count, fsdp_count = lax.axis_size("exp"), lax.axis_size("fsdp")
    devices = exp_count * fsdp_count
    rows_dev, width = tokens.shape
    experts, depth, _ = gate_weight.shape
    sent = pack_rows(tokens, expert_ids, combine_weight, exp_count, fsdp_count, exp_count * experts)
    sent = sent.reshape((devices,) + sent.shape[2:])
    rows_in = lax.all_to_all(sent, BOTH, 0, 0, tiled=True).reshape(devices * rows_dev, depth + META)
    me = jnp.stack([lax.axis_index("fsdp"), lax.axis_index("exp")]).astype(jnp.int32)
    packed, info, full = gather_rows(me, rows_in, experts, exp_count * experts, 2 * UNIT)

    def routed(units, full, packed, info, gate_weight, up_weight, down_weight):
        sent, kept = project(full, packed, up_weight, units, True, 1024)
        packed, sent = lax.optimization_barrier((packed, sent))
        gate_terms = project(full, packed, gate_weight, units, False, 1024)
        came = across(sent)
        sent, stays = add_along(*to_others(*gate_terms))
        up_terms = to_others(*fold(kept, came))
        hidden = activate(stays, across(sent), *up_terms)
        other = across(hidden)
        right, left, far = from_others(hidden)
        right_other, left_other, far_other = from_others(other)
        parts = hidden, other, right, right_other, left, left_other, far, far_other
        return finish(full, me, info, parts, down_weight, 448)

    branches = [lambda *operands, units=units: routed(units, *operands) for units in range(experts, 2 * experts + 1)]
    mixed = lax.switch(jnp.sum(full), branches, full, packed, info, gate_weight, up_weight, down_weight)
    home = lax.all_to_all(mixed.reshape(devices, rows_dev, depth), BOTH, 0, 0, tiled=True)
    home = home.reshape(exp_count, fsdp_count, rows_dev, depth).astype(jnp.float32)
    return jnp.sum(home, axis=0).astype(jnp.bfloat16).transpose(1, 0, 2).reshape(rows_dev, width)


def solution(mesh):
    return jax.shard_map(
        on_device,
        mesh=mesh,
        in_specs=(
            P(BOTH, None),
            P(BOTH, None),
            P(BOTH, None),
            P("exp", "fsdp", None),
            P("exp", "fsdp", None),
            P("exp", "fsdp", None),
        ),
        out_specs=P(BOTH, None),
        check_vma=False,
    )
```

```python
import jax
import jax.numpy as jnp
from jax import lax
from jax.experimental import pallas as pl
from jax.experimental.pallas import tpu as pltpu
from jax.sharding import PartitionSpec as P

ROUTE_SCALE = 2.827
META = 128
UNIT = 128
RING = 4
BOTH = ("exp", "fsdp")


def params(mib):
    return pltpu.CompilerParams(vmem_limit_bytes=mib * 1024 * 1024)


def dot(a, b, dims):
    return lax.dot_general(a, b, (dims, ((), ())), preferred_element_type=jnp.float32)


def pack_rows(tokens, expert_ids, combine_weight, exp_count, fsdp_count, experts):
    rows, width = tokens.shape
    depth = width // fsdp_count

    def body(tokens_hbm, ids_hbm, weight_hbm, out_ref, tokens_ref, ids_ref, weight_ref, sems):
        moves = [
            pltpu.make_async_copy(source, target, sems.at[index])
            for index, (source, target) in enumerate(
                ((ids_hbm, ids_ref), (weight_hbm, weight_ref), (tokens_hbm, tokens_ref))
            )
        ]
        for move in moves:
            move.start()
        for move in moves:
            move.wait()
        ids, weight = ids_ref[...], weight_ref[...]
        gates = ROUTE_SCALE * weight / jnp.sum(weight, axis=1, keepdims=True)
        column = lax.broadcasted_iota(jnp.int32, (rows, META), 1)
        hits = jnp.zeros((rows, META), jnp.float32)
        high_low = jnp.zeros((rows, META), jnp.float32)
        for k in range(ids.shape[1]):
            named, gate = ids[:, k : k + 1], gates[:, k : k + 1]
            high = gate.astype(jnp.bfloat16).astype(jnp.float32)
            hits = jnp.where(column == named, 1.0, hits)
            high_low = jnp.where(column == named + experts, high, high_low)
            high_low = jnp.where(column == named + 2 * experts, gate - high, high_low)
        meta = jnp.where(column < experts, hits, high_low).astype(jnp.bfloat16)
        for f in range(fsdp_count):
            block = jnp.concatenate([tokens_ref[:, f * depth : (f + 1) * depth], meta], axis=1)
            for e in range(exp_count):
                out_ref[e, f] = block

    return pl.pallas_call(
        body,
        out_shape=jax.ShapeDtypeStruct((exp_count, fsdp_count, rows, depth + META), jnp.bfloat16),
        in_specs=[pl.BlockSpec(memory_space=pltpu.HBM)] * 3,
        scratch_shapes=[
            pltpu.VMEM(tokens.shape, tokens.dtype),
            pltpu.VMEM(expert_ids.shape, expert_ids.dtype),
            pltpu.VMEM(combine_weight.shape, combine_weight.dtype),
            pltpu.SemaphoreType.DMA((3,)),
        ],
        compiler_params=params(60),
    )(tokens, expert_ids, combine_weight)


def position(target, me):
    across = (target // RING + me // RING) % 2
    along = (target + 2 * RING - me) % RING
    return jnp.where(along < 2, along, 5 - along) * 2 + across


def gather_rows(me, rows_in, experts, total, slots):
    rows, depth = rows_in.shape[0], rows_in.shape[1] - META
    part = UNIT // (2 * RING)

    def body(me_ref, rows_ref, out_ref, info_ref, full_ref):
        meta = rows_ref[:, depth:]
        before = lax.broadcasted_iota(jnp.int32, (rows, rows), 1) < lax.broadcasted_iota(jnp.int32, (rows, rows), 0)
        source = lax.broadcasted_iota(jnp.int32, (META, META), 0)
        target = lax.broadcasted_iota(jnp.int32, (META, META), 1)
        wanted = target // experts * total + me_ref[1] * experts + target % experts
        chosen = ((source == wanted) & (target < 3 * experts)).astype(jnp.bfloat16)
        meta = dot(meta, chosen, ((1,), (0,)))
        rank = dot(before.astype(jnp.bfloat16), meta.astype(jnp.bfloat16), ((1,), (0,)))
        column = lax.broadcasted_iota(jnp.int32, (rows, META), 1)
        info = jnp.zeros((rows, META), jnp.float32)
        for index in range(experts):
            hit = meta[:, index : index + 1]
            slot = jnp.where(hit > 0.5, rank[:, index : index + 1], -1.0)
            gate = meta[:, experts + index : experts + index + 1] + meta[:, 2 * experts + index : 2 * experts + index + 1]
            info = jnp.where(column == index, slot, jnp.where(column == experts + index, gate, info))
            place = slot.astype(jnp.int32) == lax.broadcasted_iota(jnp.int32, (rows, slots), 1)
            value = dot(place.astype(jnp.bfloat16), rows_ref[:, :depth], ((0,), (0,))).astype(jnp.bfloat16)
            for block in range(slots // part):
                first = block * part // UNIT * UNIT + position(block % (2 * RING), me_ref[0]) * part
                out_ref[index, pl.ds(pl.multiple_of(first, part), part)] = value[block * part : (block + 1) * part]
            full_ref[index] = (jnp.sum(hit) > UNIT).astype(jnp.int32)
        info_ref[...] = info

    return pl.pallas_call(
        body,
        out_shape=(
            jax.ShapeDtypeStruct((experts, slots, depth), jnp.bfloat16),
            jax.ShapeDtypeStruct((rows, META), jnp.float32),
            jax.ShapeDtypeStruct((experts,), jnp.int32),
        ),
        out_specs=(
            pl.BlockSpec(memory_space=pltpu.VMEM),
            pl.BlockSpec(memory_space=pltpu.VMEM),
            pl.BlockSpec(memory_space=pltpu.SMEM),
        ),
        in_specs=[pl.BlockSpec(memory_space=pltpu.SMEM), pl.BlockSpec(memory_space=pltpu.VMEM)],
        compiler_params=params(32),
    )(me, rows_in)


def extra_unit(units, experts, local):
    return experts + local if units == 2 * experts else experts


def project(full, packed, weight, units, z_first, tile):
    experts, depth, width = weight.shape
    slots = packed.shape[1]
    part = UNIT // (2 * RING)

    def body(full_ref, packed_ref, weight_ref, *outs):
        column = pl.ds(pl.multiple_of(pl.program_id(0) * tile, tile), tile)
        local = pl.program_id(1)

        def put(unit, value):
            value = value.reshape(2 * RING, part, tile)
            for order in range(RING):
                if z_first:
                    sent, own, kept = outs
                    kept[order, unit, :, column] = value[2 * order]
                    if order == 0:
                        own[unit, :, column] = value[1]
                    else:
                        sent[order - 1, unit, :, column] = value[2 * order + 1]
                else:
                    outs[order][:, unit, :, column] = value[2 * order : 2 * order + 2]

        @pl.when(full_ref[local] == 0)
        def _():
            put(local, dot(packed_ref[local, :UNIT], weight_ref[0], ((1,), (0,))).astype(jnp.bfloat16))

        if units > experts:

            @pl.when(full_ref[local] != 0)
            def _():
                value = dot(packed_ref[local], weight_ref[0], ((1,), (0,))).astype(jnp.bfloat16)
                put(local, value[:UNIT])
                put(extra_unit(units, experts, local), value[UNIT:])

    block = (units, part, width)
    shapes = [(RING - 1,) + block, block, (RING,) + block] if z_first else [(2,) + block] * RING
    return pl.pallas_call(
        body,
        grid=(width // tile, experts),
        out_shape=tuple(jax.ShapeDtypeStruct(shape, jnp.bfloat16) for shape in shapes),
        in_specs=[
            pl.BlockSpec(memory_space=pltpu.SMEM),
            pl.BlockSpec(memory_space=pltpu.VMEM),
            pl.BlockSpec((1, depth, tile), lambda n, e: (e, 0, n)),
        ],
        out_specs=tuple(pl.BlockSpec(memory_space=pltpu.VMEM) for _ in shapes),
        compiler_params=params(32),
        cost_estimate=pl.CostEstimate(
            flops=2 * units * UNIT * depth * width,
            bytes_accessed=2 * experts * depth * width + 2 * units * UNIT * width,
            transcendentals=0,
        ),
    )(full, packed, weight)


def in_pieces(shape, piece, body):
    units, _, width = shape

    def step(index, carry):
        body(index // (width // piece), pl.ds(pl.multiple_of(index % (width // piece) * piece, piece), piece))
        return carry

    lax.fori_loop(0, units * (width // piece), step, 0)


def whole_call(body, shapes, *operands):
    return pl.pallas_call(
        body,
        out_shape=tuple(jax.ShapeDtypeStruct(shape, kind) for shape, kind in shapes),
        in_specs=[pl.BlockSpec(memory_space=pltpu.VMEM)] * len(operands),
        out_specs=tuple(pl.BlockSpec(memory_space=pltpu.VMEM) for _ in shapes),
        compiler_params=params(32),
    )(*operands)


def wide(value):
    return value.astype(jnp.float32)


def fold(kept, came):
    block = kept.shape[1:]

    def body(kept_ref, came_ref, *outs):
        for order, out_ref in enumerate(outs):

            def piece(unit, column):
                total = wide(kept_ref[order + 1, unit, :, column]) + wide(came_ref[order, unit, :, column])
                out_ref[unit, :, column] = total.astype(jnp.bfloat16)

            in_pieces(block, 512, piece)

    return whole_call(body, [(block, jnp.bfloat16)] * (RING - 1), kept, came)


def add_along(*terms):
    block = terms[0].shape[1:]

    def body(*refs):
        for side, out_ref in ((1, refs[-2]), (0, refs[-1])):

            def piece(unit, column):
                total = sum(wide(ref[side, unit, :, column]) for ref in refs[1:-2])
                out_ref[unit, :, column] = (total + wide(refs[0][side, unit, :, column])).astype(out_ref.dtype)

            in_pieces(block, 512, piece)

    return whole_call(body, [(block, jnp.bfloat16), (block, jnp.float32)], *terms)


def activate(stays, came, kept, *terms):
    block = stays.shape

    def body(stays_ref, came_ref, kept_ref, *refs):
        def piece(unit, column):
            gate = stays_ref[unit, :, column] + wide(came_ref[unit, :, column])
            up = sum(wide(ref[unit, :, column]) for ref in refs[:-1]) + wide(kept_ref[0, unit, :, column])
            refs[-1][unit, :, column] = (gate / (1.0 + jnp.exp(-gate)) * up).astype(jnp.bfloat16)

        in_pieces(block, 512, piece)

    return whole_call(body, [(block, jnp.bfloat16)], stays, came, kept, *terms)[0]


def along(value, step):
    return lax.ppermute(value, "fsdp", [(i, i // RING * RING + (i + step) % RING) for i in range(2 * RING)])


def across(value):
    return lax.ppermute(value, "fsdp", [(i, (i + RING) % (2 * RING)) for i in range(2 * RING)])


def to_others(right, left, far):
    return along(right, 1), along(left, -1), along(far, 2)


def finish(full, me, info, parts, down_weight, tile):
    units, part, width = parts[0].shape
    experts, features = down_weight.shape[:2]
    rows = info.shape[0]
    count = len(parts)

    def body(full_ref, me_ref, info_ref, *refs):
        part_refs, (down_ref, out_ref, hidden, total, mixed) = refs[:count], refs[count:]
        local = pl.program_id(0)

        @pl.when(local == 0)
        def _():
            mixed[...] = jnp.zeros_like(mixed)

        def put(slots):
            for index, ref in enumerate(part_refs):
                order, side = index // 2, index % 2
                step = (0, 1, RING - 1, 2)[order]
                target = (me_ref[0] // RING + side) % 2 * RING + (me_ref[0] + step) % RING
                for first in range(0, slots, UNIT):
                    unit = extra_unit(units, experts, local) if first else local
                    hidden[pl.ds(pl.multiple_of(target * part + first, part), part)] = ref[unit]

            def step(index, carry):
                chosen = pl.ds(pl.multiple_of(index * tile, tile), tile)
                value = dot(down_ref[local, chosen], hidden[:slots], ((1,), (1,)))
                total[chosen, :slots] = value.astype(jnp.bfloat16)
                return carry

            lax.fori_loop(0, features // tile, step, 0)
            slot = jnp.where(local == 0, info_ref[:, :1], info_ref[:, 1:2])
            gate = jnp.where(local == 0, info_ref[:, 2:3], info_ref[:, 3:4])
            place = slot.astype(jnp.int32) == lax.broadcasted_iota(jnp.int32, (rows, slots), 1)
            mixed[...] += dot(place.astype(jnp.bfloat16), total[:, :slots], ((1,), (1,))) * gate

        @pl.when(full_ref[local] == 0)
        def _():
            put(UNIT)

        if units > experts:

            @pl.when(full_ref[local] != 0)
            def _():
                put(2 * UNIT)

        @pl.when(local == experts - 1)
        def _():
            out_ref[...] = mixed[...].astype(jnp.bfloat16)

    scalars, whole = pl.BlockSpec(memory_space=pltpu.SMEM), pl.BlockSpec(memory_space=pltpu.VMEM)
    return pl.pallas_call(
        body,
        grid=(experts,),
        out_shape=jax.ShapeDtypeStruct((rows, features), jnp.bfloat16),
        in_specs=[scalars, scalars] + [whole] * (count + 2),
        out_specs=whole,
        scratch_shapes=[
            pltpu.VMEM((2 * UNIT, width), jnp.bfloat16),
            pltpu.VMEM((features, 2 * UNIT), jnp.bfloat16),
            pltpu.VMEM((rows, features), jnp.float32),
        ],
        compiler_params=params(24),
        cost_estimate=pl.CostEstimate(
            flops=2 * units * UNIT * features * width,
            bytes_accessed=2 * experts * features * width + 2 * units * UNIT * width,
            transcendentals=0,
        ),
    )(full, me, info, *parts, down_weight)


def on_device(tokens, expert_ids, combine_weight, gate_weight, up_weight, down_weight):
    exp_count, fsdp_count = lax.axis_size("exp"), lax.axis_size("fsdp")
    devices = exp_count * fsdp_count
    rows_dev, width = tokens.shape
    experts, depth, _ = gate_weight.shape
    sent = pack_rows(tokens, expert_ids, combine_weight, exp_count, fsdp_count, exp_count * experts)
    sent = sent.reshape((devices,) + sent.shape[2:])
    rows_in = lax.all_to_all(sent, BOTH, 0, 0, tiled=True).reshape(devices * rows_dev, depth + META)
    me = jnp.stack([lax.axis_index("fsdp"), lax.axis_index("exp")]).astype(jnp.int32)
    packed, info, full = gather_rows(me, rows_in, experts, exp_count * experts, 2 * UNIT)

    def routed(units, full, packed, info, gate_weight, up_weight, down_weight):
        sent, own, kept = project(full, packed, up_weight, units, True, 1024)
        packed, sent = lax.optimization_barrier((packed, sent))
        gate_kept, *gate_terms = project(full, packed, gate_weight, units, False, 1024)
        came = across(sent)
        own = across(own)
        gate_terms = to_others(*gate_terms)
        up_terms = fold(kept, came)
        gate_kept, up_terms = lax.optimization_barrier((gate_kept, up_terms))
        up_terms = to_others(*up_terms)
        sent, stays = add_along(gate_kept, *gate_terms)
        hidden = activate(stays, across(sent), kept, own, *up_terms)
        other = across(hidden)
        right, left, far = along(hidden, -1), along(hidden, 1), along(hidden, 2)
        right_other, left_other, far_other = along(other, -1), along(other, 1), across(far)
        parts = hidden, other, right, right_other, left, left_other, far, far_other
        return finish(full, me, info, parts, down_weight, 448)

    order = (experts + 1, experts + 2, experts)
    branches = [lambda *operands, units=units: routed(units, *operands) for units in order]
    number = (jnp.sum(full) + len(order) - 1) % len(order)
    mixed = lax.switch(number, branches, full, packed, info, gate_weight, up_weight, down_weight)
    home = lax.all_to_all(mixed.reshape(devices, rows_dev, depth), BOTH, 0, 0, tiled=True)
    home = home.reshape(exp_count, fsdp_count, rows_dev, depth).astype(jnp.float32)
    return jnp.sum(home, axis=0).astype(jnp.bfloat16).transpose(1, 0, 2).reshape(rows_dev, width)


def solution(mesh):
    return jax.shard_map(
        on_device,
        mesh=mesh,
        in_specs=(
            P(BOTH, None),
            P(BOTH, None),
            P(BOTH, None),
            P("exp", "fsdp", None),
            P("exp", "fsdp", None),
            P("exp", "fsdp", None),
        ),
        out_specs=P(BOTH, None),
        check_vma=False,
    )
```

```python
import jax
import jax.numpy as jnp
from jax import lax
from jax.experimental import pallas as pl
from jax.experimental.pallas import tpu as pltpu
from jax.sharding import PartitionSpec as P

ROUTE_SCALE = 2.827
META = 128
UNIT = 128
RING = 4
BOTH = ("exp", "fsdp")


def params(mib):
    return pltpu.CompilerParams(vmem_limit_bytes=mib * 1024 * 1024)


def dot(a, b, dims):
    return lax.dot_general(a, b, (dims, ((), ())), preferred_element_type=jnp.float32)


def pack_rows(tokens, expert_ids, combine_weight, exp_count, fsdp_count, experts):
    rows, width = tokens.shape
    depth = width // fsdp_count

    def body(tokens_hbm, ids_hbm, weight_hbm, out_ref, tokens_ref, ids_ref, weight_ref, sems):
        moves = [
            pltpu.make_async_copy(source, target, sems.at[index])
            for index, (source, target) in enumerate(
                ((ids_hbm, ids_ref), (weight_hbm, weight_ref), (tokens_hbm, tokens_ref))
            )
        ]
        for move in moves:
            move.start()
        for move in moves:
            move.wait()
        ids, weight = ids_ref[...], weight_ref[...]
        gates = ROUTE_SCALE * weight / jnp.sum(weight, axis=1, keepdims=True)
        column = lax.broadcasted_iota(jnp.int32, (rows, META), 1)
        hits = jnp.zeros((rows, META), jnp.float32)
        high_low = jnp.zeros((rows, META), jnp.float32)
        for k in range(ids.shape[1]):
            named, gate = ids[:, k : k + 1], gates[:, k : k + 1]
            high = gate.astype(jnp.bfloat16).astype(jnp.float32)
            hits = jnp.where(column == named, 1.0, hits)
            high_low = jnp.where(column == named + experts, high, high_low)
            high_low = jnp.where(column == named + 2 * experts, gate - high, high_low)
        meta = jnp.where(column < experts, hits, high_low).astype(jnp.bfloat16)
        for f in range(fsdp_count):
            block = jnp.concatenate([tokens_ref[:, f * depth : (f + 1) * depth], meta], axis=1)
            for e in range(exp_count):
                out_ref[e, f] = block

    return pl.pallas_call(
        body,
        out_shape=jax.ShapeDtypeStruct((exp_count, fsdp_count, rows, depth + META), jnp.bfloat16),
        in_specs=[pl.BlockSpec(memory_space=pltpu.HBM)] * 3,
        scratch_shapes=[
            pltpu.VMEM(tokens.shape, tokens.dtype),
            pltpu.VMEM(expert_ids.shape, expert_ids.dtype),
            pltpu.VMEM(combine_weight.shape, combine_weight.dtype),
            pltpu.SemaphoreType.DMA((3,)),
        ],
        compiler_params=params(60),
    )(tokens, expert_ids, combine_weight)


def position(target, me):
    across = (target // RING + me // RING) % 2
    along = (target + 2 * RING - me) % RING
    return jnp.where(along < 2, along, 5 - along) * 2 + across


def gather_rows(me, rows_in, experts, total, slots):
    rows, depth = rows_in.shape[0], rows_in.shape[1] - META
    part = UNIT // (2 * RING)

    def body(me_ref, rows_ref, out_ref, info_ref, full_ref):
        meta = rows_ref[:, depth:]
        before = lax.broadcasted_iota(jnp.int32, (rows, rows), 1) < lax.broadcasted_iota(jnp.int32, (rows, rows), 0)
        source = lax.broadcasted_iota(jnp.int32, (META, META), 0)
        target = lax.broadcasted_iota(jnp.int32, (META, META), 1)
        wanted = target // experts * total + me_ref[1] * experts + target % experts
        chosen = ((source == wanted) & (target < 3 * experts)).astype(jnp.bfloat16)
        meta = dot(meta, chosen, ((1,), (0,)))
        rank = dot(before.astype(jnp.bfloat16), meta.astype(jnp.bfloat16), ((1,), (0,)))
        column = lax.broadcasted_iota(jnp.int32, (rows, META), 1)
        info = jnp.zeros((rows, META), jnp.float32)
        for index in range(experts):
            hit = meta[:, index : index + 1]
            slot = jnp.where(hit > 0.5, rank[:, index : index + 1], -1.0)
            gate = meta[:, experts + index : experts + index + 1] + meta[:, 2 * experts + index : 2 * experts + index + 1]
            info = jnp.where(column == index, slot, jnp.where(column == experts + index, gate, info))
            place = slot.astype(jnp.int32) == lax.broadcasted_iota(jnp.int32, (rows, slots), 1)
            value = dot(place.astype(jnp.bfloat16), rows_ref[:, :depth], ((0,), (0,))).astype(jnp.bfloat16)
            for block in range(slots // part):
                first = block * part // UNIT * UNIT + position(block % (2 * RING), me_ref[0]) * part
                out_ref[index, pl.ds(pl.multiple_of(first, part), part)] = value[block * part : (block + 1) * part]
            full_ref[index] = (jnp.sum(hit) > UNIT).astype(jnp.int32)
        info_ref[...] = info

    return pl.pallas_call(
        body,
        out_shape=(
            jax.ShapeDtypeStruct((experts, slots, depth), jnp.bfloat16),
            jax.ShapeDtypeStruct((rows, META), jnp.float32),
            jax.ShapeDtypeStruct((experts,), jnp.int32),
        ),
        out_specs=(
            pl.BlockSpec(memory_space=pltpu.VMEM),
            pl.BlockSpec(memory_space=pltpu.VMEM),
            pl.BlockSpec(memory_space=pltpu.SMEM),
        ),
        in_specs=[pl.BlockSpec(memory_space=pltpu.SMEM), pl.BlockSpec(memory_space=pltpu.VMEM)],
        compiler_params=params(32),
    )(me, rows_in)


def extra_unit(units, experts, local):
    return experts + local if units == 2 * experts else experts


def project(full, packed, weight, units, z_first, tile):
    experts, depth, width = weight.shape
    slots = packed.shape[1]
    part = UNIT // (2 * RING)

    def body(full_ref, packed_ref, weight_ref, *outs):
        column = pl.ds(pl.multiple_of(pl.program_id(0) * tile, tile), tile)
        local = pl.program_id(1)

        def put(unit, value):
            value = value.reshape(2 * RING, part, tile)
            for order in range(RING):
                if z_first:
                    sent, own, kept = outs
                    kept[order, unit, :, column] = value[2 * order]
                    if order == 0:
                        own[unit, :, column] = value[1]
                    else:
                        sent[order - 1, unit, :, column] = value[2 * order + 1]
                else:
                    outs[order][:, unit, :, column] = value[2 * order : 2 * order + 2]

        @pl.when(full_ref[local] == 0)
        def _():
            put(local, dot(packed_ref[local, :UNIT], weight_ref[0], ((1,), (0,))).astype(jnp.bfloat16))

        if units > experts:

            @pl.when(full_ref[local] != 0)
            def _():
                value = dot(packed_ref[local], weight_ref[0], ((1,), (0,))).astype(jnp.bfloat16)
                put(local, value[:UNIT])
                put(extra_unit(units, experts, local), value[UNIT:])

    block = (units, part, width)
    shapes = [(RING - 1,) + block, block, (RING,) + block] if z_first else [(2,) + block] * RING
    return pl.pallas_call(
        body,
        grid=(width // tile, experts),
        out_shape=tuple(jax.ShapeDtypeStruct(shape, jnp.bfloat16) for shape in shapes),
        in_specs=[
            pl.BlockSpec(memory_space=pltpu.SMEM),
            pl.BlockSpec(memory_space=pltpu.VMEM),
            pl.BlockSpec((1, depth, tile), lambda n, e: (e, 0, n)),
        ],
        out_specs=tuple(pl.BlockSpec(memory_space=pltpu.VMEM) for _ in shapes),
        compiler_params=params(32),
        cost_estimate=pl.CostEstimate(
            flops=2 * units * UNIT * depth * width,
            bytes_accessed=2 * experts * depth * width + 2 * units * UNIT * width,
            transcendentals=0,
        ),
    )(full, packed, weight)


def in_pieces(shape, piece, body):
    units, _, width = shape

    def step(index, carry):
        body(index // (width // piece), pl.ds(pl.multiple_of(index % (width // piece) * piece, piece), piece))
        return carry

    lax.fori_loop(0, units * (width // piece), step, 0)


def whole_call(body, shapes, *operands):
    return pl.pallas_call(
        body,
        out_shape=tuple(jax.ShapeDtypeStruct(shape, kind) for shape, kind in shapes),
        in_specs=[pl.BlockSpec(memory_space=pltpu.VMEM)] * len(operands),
        out_specs=tuple(pl.BlockSpec(memory_space=pltpu.VMEM) for _ in shapes),
        compiler_params=params(32),
    )(*operands)


def wide(value):
    return value.astype(jnp.float32)


def fold(kept, came):
    block = kept.shape[1:]

    def body(kept_ref, came_ref, *outs):
        for order, out_ref in enumerate(outs):

            def piece(unit, column):
                total = wide(kept_ref[order + 1, unit, :, column]) + wide(came_ref[order, unit, :, column])
                out_ref[unit, :, column] = total.astype(jnp.bfloat16)

            in_pieces(block, 512, piece)

    return whole_call(body, [(block, jnp.bfloat16)] * (RING - 1), kept, came)


def add_along(*terms):
    block = terms[0].shape[1:]

    def body(*refs):
        for side, out_ref in ((1, refs[-2]), (0, refs[-1])):

            def piece(unit, column):
                total = sum(wide(ref[side, unit, :, column]) for ref in refs[1:-2])
                out_ref[unit, :, column] = (total + wide(refs[0][side, unit, :, column])).astype(out_ref.dtype)

            in_pieces(block, 512, piece)

    return whole_call(body, [(block, jnp.bfloat16), (block, jnp.float32)], *terms)


def activate(stays, came, kept, *terms):
    block = stays.shape

    def body(stays_ref, came_ref, kept_ref, *refs):
        def piece(unit, column):
            gate = stays_ref[unit, :, column] + wide(came_ref[unit, :, column])
            up = sum(wide(ref[unit, :, column]) for ref in refs[:-1]) + wide(kept_ref[0, unit, :, column])
            refs[-1][unit, :, column] = (gate / (1.0 + jnp.exp(-gate)) * up).astype(jnp.bfloat16)

        in_pieces(block, 512, piece)

    return whole_call(body, [(block, jnp.bfloat16)], stays, came, kept, *terms)[0]


def along(value, step):
    return lax.ppermute(value, "fsdp", [(i, i // RING * RING + (i + step) % RING) for i in range(2 * RING)])


def across(value):
    return lax.ppermute(value, "fsdp", [(i, (i + RING) % (2 * RING)) for i in range(2 * RING)])


def to_others(right, left, far):
    return along(right, 1), along(left, -1), along(far, 2)


def finish(full, me, info, parts, down_weight, tile):
    units, part, width = parts[0].shape
    experts, features = down_weight.shape[:2]
    rows = info.shape[0]
    count = len(parts)

    def body(full_ref, me_ref, info_ref, *refs):
        part_refs, (down_ref, out_ref, hidden, total, mixed) = refs[:count], refs[count:]
        local = pl.program_id(0)

        @pl.when(local == 0)
        def _():
            mixed[...] = jnp.zeros_like(mixed)

        def put(slots):
            for index, ref in enumerate(part_refs):
                order, side = index // 2, index % 2
                step = (0, 1, RING - 1, 2)[order]
                target = (me_ref[0] // RING + side) % 2 * RING + (me_ref[0] + step) % RING
                for first in range(0, slots, UNIT):
                    unit = extra_unit(units, experts, local) if first else local
                    hidden[pl.ds(pl.multiple_of(target * part + first, part), part)] = ref[unit]

            def step(index, carry):
                chosen = pl.ds(pl.multiple_of(index * tile, tile), tile)
                value = dot(down_ref[local, chosen], hidden[:slots], ((1,), (1,)))
                total[chosen, :slots] = value.astype(jnp.bfloat16)
                return carry

            lax.fori_loop(0, features // tile, step, 0)
            slot = jnp.where(local == 0, info_ref[:, :1], info_ref[:, 1:2])
            gate = jnp.where(local == 0, info_ref[:, 2:3], info_ref[:, 3:4])
            place = slot.astype(jnp.int32) == lax.broadcasted_iota(jnp.int32, (rows, slots), 1)
            mixed[...] += dot(place.astype(jnp.bfloat16), total[:, :slots], ((1,), (1,))) * gate

        @pl.when(full_ref[local] == 0)
        def _():
            put(UNIT)

        if units > experts:

            @pl.when(full_ref[local] != 0)
            def _():
                put(2 * UNIT)

        @pl.when(local == experts - 1)
        def _():
            out_ref[...] = mixed[...].astype(jnp.bfloat16)

    scalars, whole = pl.BlockSpec(memory_space=pltpu.SMEM), pl.BlockSpec(memory_space=pltpu.VMEM)
    return pl.pallas_call(
        body,
        grid=(experts,),
        out_shape=jax.ShapeDtypeStruct((rows, features), jnp.bfloat16),
        in_specs=[scalars, scalars] + [whole] * (count + 2),
        out_specs=whole,
        scratch_shapes=[
            pltpu.VMEM((2 * UNIT, width), jnp.bfloat16),
            pltpu.VMEM((features, 2 * UNIT), jnp.bfloat16),
            pltpu.VMEM((rows, features), jnp.float32),
        ],
        compiler_params=params(24),
        cost_estimate=pl.CostEstimate(
            flops=2 * units * UNIT * features * width,
            bytes_accessed=2 * experts * features * width + 2 * units * UNIT * width,
            transcendentals=0,
        ),
    )(full, me, info, *parts, down_weight)


def on_device(tokens, expert_ids, combine_weight, gate_weight, up_weight, down_weight):
    exp_count, fsdp_count = lax.axis_size("exp"), lax.axis_size("fsdp")
    devices = exp_count * fsdp_count
    rows_dev, width = tokens.shape
    experts, depth, _ = gate_weight.shape
    sent = pack_rows(tokens, expert_ids, combine_weight, exp_count, fsdp_count, exp_count * experts)
    sent = sent.reshape((devices,) + sent.shape[2:])
    rows_in = lax.all_to_all(sent, BOTH, 0, 0, tiled=True).reshape(devices * rows_dev, depth + META)
    me = jnp.stack([lax.axis_index("fsdp"), lax.axis_index("exp")]).astype(jnp.int32)
    packed, info, full = gather_rows(me, rows_in, experts, exp_count * experts, 2 * UNIT)

    def routed(units, full, packed, info, gate_weight, up_weight, down_weight):
        sent, own, kept = project(full, packed, up_weight, units, True, 2048)
        packed, sent = lax.optimization_barrier((packed, sent))
        gate_kept, *gate_terms = project(full, packed, gate_weight, units, False, 2048)
        came = across(sent)
        own = across(own)
        gate_terms = to_others(*gate_terms)
        up_terms = fold(kept, came)
        gate_kept, up_terms = lax.optimization_barrier((gate_kept, up_terms))
        up_terms = to_others(*up_terms)
        sent, stays = add_along(gate_kept, *gate_terms)
        hidden = activate(stays, across(sent), kept, own, *up_terms)
        other = across(hidden)
        right, left, far = along(hidden, -1), along(hidden, 1), along(hidden, 2)
        right_other, left_other, far_other = along(other, -1), along(other, 1), across(far)
        parts = hidden, other, right, right_other, left, left_other, far, far_other
        return finish(full, me, info, parts, down_weight, 448)

    branches = [lambda *operands, units=units: routed(units, *operands) for units in range(experts, 2 * experts + 1)]
    mixed = lax.switch(jnp.sum(full), branches, full, packed, info, gate_weight, up_weight, down_weight)
    home = lax.all_to_all(mixed.reshape(devices, rows_dev, depth), BOTH, 0, 0, tiled=True)
    home = home.reshape(exp_count, fsdp_count, rows_dev, depth).astype(jnp.float32)
    return jnp.sum(home, axis=0).astype(jnp.bfloat16).transpose(1, 0, 2).reshape(rows_dev, width)


def solution(mesh):
    return jax.shard_map(
        on_device,
        mesh=mesh,
        in_specs=(
            P(BOTH, None),
            P(BOTH, None),
            P(BOTH, None),
            P("exp", "fsdp", None),
            P("exp", "fsdp", None),
            P("exp", "fsdp", None),
        ),
        out_specs=P(BOTH, None),
        check_vma=False,
    )
```

```python
import jax
import jax.numpy as jnp
from jax import lax
from jax.experimental import pallas as pl
from jax.experimental.pallas import tpu as pltpu
from jax.sharding import PartitionSpec as P

ROUTE_SCALE = 2.827
META = 128
UNIT = 128
RING = 4
BOTH = ("exp", "fsdp")


def params(mib):
    return pltpu.CompilerParams(vmem_limit_bytes=mib * 1024 * 1024)


def dot(a, b, dims):
    return lax.dot_general(a, b, (dims, ((), ())), preferred_element_type=jnp.float32)


def pack_rows(tokens, expert_ids, combine_weight, exp_count, fsdp_count, experts):
    rows, width = tokens.shape
    depth = width // fsdp_count

    def body(tokens_hbm, ids_hbm, weight_hbm, out_ref, tokens_ref, ids_ref, weight_ref, sems):
        moves = [
            pltpu.make_async_copy(source, target, sems.at[index])
            for index, (source, target) in enumerate(
                ((ids_hbm, ids_ref), (weight_hbm, weight_ref), (tokens_hbm, tokens_ref))
            )
        ]
        for move in moves:
            move.start()
        for move in moves:
            move.wait()
        ids, weight = ids_ref[...], weight_ref[...]
        gates = ROUTE_SCALE * weight / jnp.sum(weight, axis=1, keepdims=True)
        column = lax.broadcasted_iota(jnp.int32, (rows, META), 1)
        hits = jnp.zeros((rows, META), jnp.float32)
        high_low = jnp.zeros((rows, META), jnp.float32)
        for k in range(ids.shape[1]):
            named, gate = ids[:, k : k + 1], gates[:, k : k + 1]
            high = gate.astype(jnp.bfloat16).astype(jnp.float32)
            hits = jnp.where(column == named, 1.0, hits)
            high_low = jnp.where(column == named + experts, high, high_low)
            high_low = jnp.where(column == named + 2 * experts, gate - high, high_low)
        meta = jnp.where(column < experts, hits, high_low).astype(jnp.bfloat16)
        for f in range(fsdp_count):
            block = jnp.concatenate([tokens_ref[:, f * depth : (f + 1) * depth], meta], axis=1)
            for e in range(exp_count):
                out_ref[e, f] = block

    return pl.pallas_call(
        body,
        out_shape=jax.ShapeDtypeStruct((exp_count, fsdp_count, rows, depth + META), jnp.bfloat16),
        in_specs=[pl.BlockSpec(memory_space=pltpu.HBM)] * 3,
        scratch_shapes=[
            pltpu.VMEM(tokens.shape, tokens.dtype),
            pltpu.VMEM(expert_ids.shape, expert_ids.dtype),
            pltpu.VMEM(combine_weight.shape, combine_weight.dtype),
            pltpu.SemaphoreType.DMA((3,)),
        ],
        compiler_params=params(60),
    )(tokens, expert_ids, combine_weight)


def position(target, me):
    across = (target // RING + me // RING) % 2
    along = (target + 2 * RING - me) % RING
    return jnp.where(along < 2, along, 5 - along) * 2 + across


def gather_rows(me, rows_in, experts, total, slots):
    rows, depth = rows_in.shape[0], rows_in.shape[1] - META
    part = UNIT // (2 * RING)

    def body(me_ref, rows_ref, out_ref, info_ref, full_ref):
        meta = rows_ref[:, depth:]
        before = lax.broadcasted_iota(jnp.int32, (rows, rows), 1) < lax.broadcasted_iota(jnp.int32, (rows, rows), 0)
        source = lax.broadcasted_iota(jnp.int32, (META, META), 0)
        target = lax.broadcasted_iota(jnp.int32, (META, META), 1)
        wanted = target // experts * total + me_ref[1] * experts + target % experts
        chosen = ((source == wanted) & (target < 3 * experts)).astype(jnp.bfloat16)
        meta = dot(meta, chosen, ((1,), (0,)))
        rank = dot(before.astype(jnp.bfloat16), meta.astype(jnp.bfloat16), ((1,), (0,)))
        column = lax.broadcasted_iota(jnp.int32, (rows, META), 1)
        info = jnp.zeros((rows, META), jnp.float32)
        for index in range(experts):
            hit = meta[:, index : index + 1]
            slot = jnp.where(hit > 0.5, rank[:, index : index + 1], -1.0)
            gate = meta[:, experts + index : experts + index + 1] + meta[:, 2 * experts + index : 2 * experts + index + 1]
            info = jnp.where(column == index, slot, jnp.where(column == experts + index, gate, info))
            place = slot.astype(jnp.int32) == lax.broadcasted_iota(jnp.int32, (rows, slots), 1)
            value = dot(place.astype(jnp.bfloat16), rows_ref[:, :depth], ((0,), (0,))).astype(jnp.bfloat16)
            for block in range(slots // part):
                first = block * part // UNIT * UNIT + position(block % (2 * RING), me_ref[0]) * part
                out_ref[index, pl.ds(pl.multiple_of(first, part), part)] = value[block * part : (block + 1) * part]
            full_ref[index] = (jnp.sum(hit) > UNIT).astype(jnp.int32)
        info_ref[...] = info

    return pl.pallas_call(
        body,
        out_shape=(
            jax.ShapeDtypeStruct((experts, slots, depth), jnp.bfloat16),
            jax.ShapeDtypeStruct((rows, META), jnp.float32),
            jax.ShapeDtypeStruct((experts,), jnp.int32),
        ),
        out_specs=(
            pl.BlockSpec(memory_space=pltpu.VMEM),
            pl.BlockSpec(memory_space=pltpu.VMEM),
            pl.BlockSpec(memory_space=pltpu.SMEM),
        ),
        in_specs=[pl.BlockSpec(memory_space=pltpu.SMEM), pl.BlockSpec(memory_space=pltpu.VMEM)],
        compiler_params=params(32),
    )(me, rows_in)


def extra_unit(units, experts, local):
    return experts + local if units == 2 * experts else experts


def project(full, packed, weight, units, z_first, tile):
    experts, depth, width = weight.shape
    slots = packed.shape[1]
    part = UNIT // (2 * RING)

    def body(full_ref, packed_ref, weight_ref, *outs):
        column = pl.ds(pl.multiple_of(pl.program_id(0) * tile, tile), tile)
        local = pl.program_id(1)

        def put(unit, value):
            value = value.reshape(2 * RING, part, tile)
            for order in range(RING):
                if z_first:
                    sent, own, kept = outs
                    kept[order, unit, :, column] = value[2 * order]
                    if order == 0:
                        own[unit, :, column] = value[1]
                    else:
                        sent[order - 1, unit, :, column] = value[2 * order + 1]
                else:
                    outs[order][:, unit, :, column] = value[2 * order : 2 * order + 2]

        if units < 2 * experts:

            @pl.when(full_ref[local] == 0)
            def _():
                put(local, dot(packed_ref[local, :UNIT], weight_ref[0], ((1,), (0,))).astype(jnp.bfloat16))

        if units > experts:

            @pl.when(full_ref[local] != 0)
            def _():
                value = dot(packed_ref[local], weight_ref[0], ((1,), (0,))).astype(jnp.bfloat16)
                put(local, value[:UNIT])
                put(extra_unit(units, experts, local), value[UNIT:])

    block = (units, part, width)
    shapes = [(RING - 1,) + block, block, (RING,) + block] if z_first else [(2,) + block] * RING
    return pl.pallas_call(
        body,
        grid=(width // tile, experts),
        out_shape=tuple(jax.ShapeDtypeStruct(shape, jnp.bfloat16) for shape in shapes),
        in_specs=[
            pl.BlockSpec(memory_space=pltpu.SMEM),
            pl.BlockSpec(memory_space=pltpu.VMEM),
            pl.BlockSpec((1, depth, tile), lambda n, e: (e, 0, n)),
        ],
        out_specs=tuple(pl.BlockSpec(memory_space=pltpu.VMEM) for _ in shapes),
        compiler_params=params(32),
        cost_estimate=pl.CostEstimate(
            flops=2 * units * UNIT * depth * width,
            bytes_accessed=2 * experts * depth * width + 2 * units * UNIT * width,
            transcendentals=0,
        ),
    )(full, packed, weight)


def in_pieces(shape, piece, body):
    units, _, width = shape

    def step(index, carry):
        body(index // (width // piece), pl.ds(pl.multiple_of(index % (width // piece) * piece, piece), piece))
        return carry

    lax.fori_loop(0, units * (width // piece), step, 0)


def whole_call(body, shapes, *operands):
    return pl.pallas_call(
        body,
        out_shape=tuple(jax.ShapeDtypeStruct(shape, kind) for shape, kind in shapes),
        in_specs=[pl.BlockSpec(memory_space=pltpu.VMEM)] * len(operands),
        out_specs=tuple(pl.BlockSpec(memory_space=pltpu.VMEM) for _ in shapes),
        compiler_params=params(32),
    )(*operands)


def wide(value):
    return value.astype(jnp.float32)


def fold(kept, came):
    block = kept.shape[1:]

    def body(kept_ref, came_ref, *outs):
        for order, out_ref in enumerate(outs):

            def piece(unit, column):
                total = wide(kept_ref[order + 1, unit, :, column]) + wide(came_ref[order, unit, :, column])
                out_ref[unit, :, column] = total.astype(jnp.bfloat16)

            in_pieces(block, 512, piece)

    return whole_call(body, [(block, jnp.bfloat16)] * (RING - 1), kept, came)


def add_along(*terms):
    block = terms[0].shape[1:]

    def body(*refs):
        for side, out_ref in ((1, refs[-2]), (0, refs[-1])):

            def piece(unit, column):
                total = sum(wide(ref[side, unit, :, column]) for ref in refs[1:-2])
                out_ref[unit, :, column] = (total + wide(refs[0][side, unit, :, column])).astype(out_ref.dtype)

            in_pieces(block, 512, piece)

    return whole_call(body, [(block, jnp.bfloat16), (block, jnp.float32)], *terms)


def activate(stays, came, kept, *terms):
    block = stays.shape

    def body(stays_ref, came_ref, kept_ref, *refs):
        def piece(unit, column):
            gate = stays_ref[unit, :, column] + wide(came_ref[unit, :, column])
            up = sum(wide(ref[unit, :, column]) for ref in refs[:-1]) + wide(kept_ref[0, unit, :, column])
            refs[-1][unit, :, column] = (gate / (1.0 + jnp.exp(-gate)) * up).astype(jnp.bfloat16)

        in_pieces(block, 512, piece)

    return whole_call(body, [(block, jnp.bfloat16)], stays, came, kept, *terms)[0]


def along(value, step):
    return lax.ppermute(value, "fsdp", [(i, i // RING * RING + (i + step) % RING) for i in range(2 * RING)])


def across(value):
    return lax.ppermute(value, "fsdp", [(i, (i + RING) % (2 * RING)) for i in range(2 * RING)])


def to_others(right, left, far):
    return along(right, 1), along(left, -1), along(far, 2)


def finish(full, me, info, parts, down_weight, tile):
    units, part, width = parts[0].shape
    experts, features = down_weight.shape[:2]
    rows = info.shape[0]
    count = len(parts)

    def body(full_ref, me_ref, info_ref, *refs):
        part_refs, (down_ref, out_ref, hidden, total, mixed) = refs[:count], refs[count:]
        local = pl.program_id(0)

        @pl.when(local == 0)
        def _():
            mixed[...] = jnp.zeros_like(mixed)

        def put(slots):
            for index, ref in enumerate(part_refs):
                order, side = index // 2, index % 2
                step = (0, 1, RING - 1, 2)[order]
                target = (me_ref[0] // RING + side) % 2 * RING + (me_ref[0] + step) % RING
                for first in range(0, slots, UNIT):
                    unit = extra_unit(units, experts, local) if first else local
                    hidden[pl.ds(pl.multiple_of(target * part + first, part), part)] = ref[unit]

            def step(index, carry):
                chosen = pl.ds(pl.multiple_of(index * tile, tile), tile)
                value = dot(down_ref[local, chosen], hidden[:slots], ((1,), (1,)))
                total[chosen, :slots] = value.astype(jnp.bfloat16)
                return carry

            lax.fori_loop(0, features // tile, step, 0)
            slot = jnp.where(local == 0, info_ref[:, :1], info_ref[:, 1:2])
            gate = jnp.where(local == 0, info_ref[:, 2:3], info_ref[:, 3:4])
            place = slot.astype(jnp.int32) == lax.broadcasted_iota(jnp.int32, (rows, slots), 1)
            mixed[...] += dot(place.astype(jnp.bfloat16), total[:, :slots], ((1,), (1,))) * gate

        if units < 2 * experts:

            @pl.when(full_ref[local] == 0)
            def _():
                put(UNIT)

        if units > experts:

            @pl.when(full_ref[local] != 0)
            def _():
                put(2 * UNIT)

        @pl.when(local == experts - 1)
        def _():
            out_ref[...] = mixed[...].astype(jnp.bfloat16)

    scalars, whole = pl.BlockSpec(memory_space=pltpu.SMEM), pl.BlockSpec(memory_space=pltpu.VMEM)
    return pl.pallas_call(
        body,
        grid=(experts,),
        out_shape=jax.ShapeDtypeStruct((rows, features), jnp.bfloat16),
        in_specs=[scalars, scalars] + [whole] * (count + 2),
        out_specs=whole,
        scratch_shapes=[
            pltpu.VMEM((2 * UNIT, width), jnp.bfloat16),
            pltpu.VMEM((features, 2 * UNIT), jnp.bfloat16),
            pltpu.VMEM((rows, features), jnp.float32),
        ],
        compiler_params=params(24),
        cost_estimate=pl.CostEstimate(
            flops=2 * units * UNIT * features * width,
            bytes_accessed=2 * experts * features * width + 2 * units * UNIT * width,
            transcendentals=0,
        ),
    )(full, me, info, *parts, down_weight)


def on_device(tokens, expert_ids, combine_weight, gate_weight, up_weight, down_weight):
    exp_count, fsdp_count = lax.axis_size("exp"), lax.axis_size("fsdp")
    devices = exp_count * fsdp_count
    rows_dev, width = tokens.shape
    experts, depth, _ = gate_weight.shape
    sent = pack_rows(tokens, expert_ids, combine_weight, exp_count, fsdp_count, exp_count * experts)
    sent = sent.reshape((devices,) + sent.shape[2:])
    rows_in = lax.all_to_all(sent, BOTH, 0, 0, tiled=True).reshape(devices * rows_dev, depth + META)
    me = jnp.stack([lax.axis_index("fsdp"), lax.axis_index("exp")]).astype(jnp.int32)
    packed, info, full = gather_rows(me, rows_in, experts, exp_count * experts, 2 * UNIT)

    def routed(units, full, packed, info, gate_weight, up_weight, down_weight):
        sent, own, kept = project(full, packed, up_weight, units, True, 2048)
        packed, sent = lax.optimization_barrier((packed, sent))
        gate_kept, *gate_terms = project(full, packed, gate_weight, units, False, 2048)
        came = across(sent)
        own = across(own)
        gate_terms = to_others(*gate_terms)
        up_terms = fold(kept, came)
        gate_kept, up_terms = lax.optimization_barrier((gate_kept, up_terms))
        up_terms = to_others(*up_terms)
        sent, stays = add_along(gate_kept, *gate_terms)
        hidden = activate(stays, across(sent), kept, own, *up_terms)
        other = across(hidden)
        right, left, far = along(hidden, -1), along(hidden, 1), along(hidden, 2)
        right_other, left_other, far_other = along(other, -1), along(other, 1), across(far)
        parts = hidden, other, right, right_other, left, left_other, far, far_other
        return finish(full, me, info, parts, down_weight, 448)

    order = (experts + 1, 2 * experts, experts)
    branches = [lambda *operands, units=units: routed(units, *operands) for units in order]
    number = (jnp.sum(full) + len(order) - 1) % len(order)
    mixed = lax.switch(number, branches, full, packed, info, gate_weight, up_weight, down_weight)
    home = lax.all_to_all(mixed.reshape(devices, rows_dev, depth), BOTH, 0, 0, tiled=True)
    home = home.reshape(exp_count, fsdp_count, rows_dev, depth).astype(jnp.float32)
    return jnp.sum(home, axis=0).astype(jnp.bfloat16).transpose(1, 0, 2).reshape(rows_dev, width)


def solution(mesh):
    return jax.shard_map(
        on_device,
        mesh=mesh,
        in_specs=(
            P(BOTH, None),
            P(BOTH, None),
            P(BOTH, None),
            P("exp", "fsdp", None),
            P("exp", "fsdp", None),
            P("exp", "fsdp", None),
        ),
        out_specs=P(BOTH, None),
        check_vma=False,
    )
```

```python
import jax
import jax.numpy as jnp
from jax import lax
from jax.experimental import pallas as pl
from jax.experimental.pallas import tpu as pltpu
from jax.sharding import PartitionSpec as P

ROUTE_SCALE = 2.827
META = 128
UNIT = 128
RING = 4
BOTH = ("exp", "fsdp")


def params(mib):
    return pltpu.CompilerParams(vmem_limit_bytes=mib * 1024 * 1024)


def dot(a, b, dims):
    return lax.dot_general(a, b, (dims, ((), ())), preferred_element_type=jnp.float32)


def pack_rows(tokens, expert_ids, combine_weight, exp_count, fsdp_count, experts):
    rows, width = tokens.shape
    depth = width // fsdp_count

    def body(tokens_hbm, ids_hbm, weight_hbm, out_ref, tokens_ref, ids_ref, weight_ref, sems):
        moves = [
            pltpu.make_async_copy(source, target, sems.at[index])
            for index, (source, target) in enumerate(
                ((ids_hbm, ids_ref), (weight_hbm, weight_ref), (tokens_hbm, tokens_ref))
            )
        ]
        for move in moves:
            move.start()
        for move in moves:
            move.wait()
        ids, weight = ids_ref[...], weight_ref[...]
        gates = ROUTE_SCALE * weight / jnp.sum(weight, axis=1, keepdims=True)
        column = lax.broadcasted_iota(jnp.int32, (rows, META), 1)
        hits = jnp.zeros((rows, META), jnp.float32)
        high_low = jnp.zeros((rows, META), jnp.float32)
        for k in range(ids.shape[1]):
            named, gate = ids[:, k : k + 1], gates[:, k : k + 1]
            high = gate.astype(jnp.bfloat16).astype(jnp.float32)
            hits = jnp.where(column == named, 1.0, hits)
            high_low = jnp.where(column == named + experts, high, high_low)
            high_low = jnp.where(column == named + 2 * experts, gate - high, high_low)
        meta = jnp.where(column < experts, hits, high_low).astype(jnp.bfloat16)
        for f in range(fsdp_count):
            block = jnp.concatenate([tokens_ref[:, f * depth : (f + 1) * depth], meta], axis=1)
            for e in range(exp_count):
                out_ref[e, f] = block

    return pl.pallas_call(
        body,
        out_shape=jax.ShapeDtypeStruct((exp_count, fsdp_count, rows, depth + META), jnp.bfloat16),
        in_specs=[pl.BlockSpec(memory_space=pltpu.HBM)] * 3,
        scratch_shapes=[
            pltpu.VMEM(tokens.shape, tokens.dtype),
            pltpu.VMEM(expert_ids.shape, expert_ids.dtype),
            pltpu.VMEM(combine_weight.shape, combine_weight.dtype),
            pltpu.SemaphoreType.DMA((3,)),
        ],
        compiler_params=params(60),
    )(tokens, expert_ids, combine_weight)


def position(target, me):
    across = (target // RING + me // RING) % 2
    along = (target + 2 * RING - me) % RING
    return jnp.where(along < 2, along, 5 - along) * 2 + across


def gather_rows(me, rows_in, experts, total, slots):
    rows, depth = rows_in.shape[0], rows_in.shape[1] - META
    part = UNIT // (2 * RING)

    def body(me_ref, rows_ref, out_ref, info_ref, full_ref):
        meta = rows_ref[:, depth:]
        before = lax.broadcasted_iota(jnp.int32, (rows, rows), 1) < lax.broadcasted_iota(jnp.int32, (rows, rows), 0)
        source = lax.broadcasted_iota(jnp.int32, (META, META), 0)
        target = lax.broadcasted_iota(jnp.int32, (META, META), 1)
        wanted = target // experts * total + me_ref[1] * experts + target % experts
        chosen = ((source == wanted) & (target < 3 * experts)).astype(jnp.bfloat16)
        meta = dot(meta, chosen, ((1,), (0,)))
        rank = dot(before.astype(jnp.bfloat16), meta.astype(jnp.bfloat16), ((1,), (0,)))
        column = lax.broadcasted_iota(jnp.int32, (rows, META), 1)
        info = jnp.zeros((rows, META), jnp.float32)
        for index in range(experts):
            hit = meta[:, index : index + 1]
            slot = jnp.where(hit > 0.5, rank[:, index : index + 1], -1.0)
            gate = meta[:, experts + index : experts + index + 1] + meta[:, 2 * experts + index : 2 * experts + index + 1]
            info = jnp.where(column == index, slot, jnp.where(column == experts + index, gate, info))
            place = slot.astype(jnp.int32) == lax.broadcasted_iota(jnp.int32, (rows, slots), 1)
            value = dot(place.astype(jnp.bfloat16), rows_ref[:, :depth], ((0,), (0,))).astype(jnp.bfloat16)
            for block in range(slots // part):
                first = block * part // UNIT * UNIT + position(block % (2 * RING), me_ref[0]) * part
                out_ref[index, pl.ds(pl.multiple_of(first, part), part)] = value[block * part : (block + 1) * part]
            full_ref[index] = (jnp.sum(hit) > UNIT).astype(jnp.int32)
        info_ref[...] = info

    return pl.pallas_call(
        body,
        out_shape=(
            jax.ShapeDtypeStruct((experts, slots, depth), jnp.bfloat16),
            jax.ShapeDtypeStruct((rows, META), jnp.float32),
            jax.ShapeDtypeStruct((experts,), jnp.int32),
        ),
        out_specs=(
            pl.BlockSpec(memory_space=pltpu.VMEM),
            pl.BlockSpec(memory_space=pltpu.VMEM),
            pl.BlockSpec(memory_space=pltpu.SMEM),
        ),
        in_specs=[pl.BlockSpec(memory_space=pltpu.SMEM), pl.BlockSpec(memory_space=pltpu.VMEM)],
        compiler_params=params(32),
    )(me, rows_in)


def extra_unit(units, experts, local):
    return experts + local if units == 2 * experts else experts


def project(full, packed, weight, units, z_first, tile):
    experts, depth, width = weight.shape
    slots = packed.shape[1]
    part = UNIT // (2 * RING)

    def body(full_ref, packed_ref, weight_ref, *outs):
        column = pl.ds(pl.multiple_of(pl.program_id(0) * tile, tile), tile)
        local = pl.program_id(1)

        def put(unit, value):
            value = value.reshape(2 * RING, part, tile)
            for order in range(RING):
                if z_first:
                    sent, own, kept = outs
                    kept[order, unit, :, column] = value[2 * order]
                    if order == 0:
                        own[unit, :, column] = value[1]
                    else:
                        sent[order - 1, unit, :, column] = value[2 * order + 1]
                else:
                    outs[order][:, unit, :, column] = value[2 * order : 2 * order + 2]

        if units < 2 * experts:

            @pl.when(full_ref[local] == 0)
            def _():
                put(local, dot(packed_ref[local, :UNIT], weight_ref[0], ((1,), (0,))).astype(jnp.bfloat16))

        if units > experts:

            @pl.when(full_ref[local] != 0)
            def _():
                value = dot(packed_ref[local], weight_ref[0], ((1,), (0,))).astype(jnp.bfloat16)
                put(local, value[:UNIT])
                put(extra_unit(units, experts, local), value[UNIT:])

    block = (units, part, width)
    shapes = [(RING - 1,) + block, block, (RING,) + block] if z_first else [(2,) + block] * RING
    return pl.pallas_call(
        body,
        grid=(width // tile, experts),
        out_shape=tuple(jax.ShapeDtypeStruct(shape, jnp.bfloat16) for shape in shapes),
        in_specs=[
            pl.BlockSpec(memory_space=pltpu.SMEM),
            pl.BlockSpec(memory_space=pltpu.VMEM),
            pl.BlockSpec((1, depth, tile), lambda n, e: (e, 0, n)),
        ],
        out_specs=tuple(pl.BlockSpec(memory_space=pltpu.VMEM) for _ in shapes),
        compiler_params=params(32),
        cost_estimate=pl.CostEstimate(
            flops=2 * units * UNIT * depth * width,
            bytes_accessed=2 * experts * depth * width + 2 * units * UNIT * width,
            transcendentals=0,
        ),
    )(full, packed, weight)


def in_pieces(shape, piece, body):
    units, _, width = shape

    def step(index, carry):
        body(index // (width // piece), pl.ds(pl.multiple_of(index % (width // piece) * piece, piece), piece))
        return carry

    lax.fori_loop(0, units * (width // piece), step, 0)


def whole_call(body, shapes, *operands):
    return pl.pallas_call(
        body,
        out_shape=tuple(jax.ShapeDtypeStruct(shape, kind) for shape, kind in shapes),
        in_specs=[pl.BlockSpec(memory_space=pltpu.VMEM)] * len(operands),
        out_specs=tuple(pl.BlockSpec(memory_space=pltpu.VMEM) for _ in shapes),
        compiler_params=params(32),
    )(*operands)


def wide(value):
    return value.astype(jnp.float32)


def fold(kept, came):
    block = kept.shape[1:]

    def body(kept_ref, came_ref, *outs):
        for order, out_ref in enumerate(outs):

            def piece(unit, column):
                total = wide(kept_ref[order + 1, unit, :, column]) + wide(came_ref[order, unit, :, column])
                out_ref[unit, :, column] = total.astype(jnp.bfloat16)

            in_pieces(block, 512, piece)

    return whole_call(body, [(block, jnp.bfloat16)] * (RING - 1), kept, came)


def add_along(*terms):
    block = terms[0].shape[1:]

    def body(*refs):
        for side, out_ref in ((1, refs[-2]), (0, refs[-1])):

            def piece(unit, column):
                total = sum(wide(ref[side, unit, :, column]) for ref in refs[1:-2])
                out_ref[unit, :, column] = (total + wide(refs[0][side, unit, :, column])).astype(out_ref.dtype)

            in_pieces(block, 512, piece)

    return whole_call(body, [(block, jnp.bfloat16), (block, jnp.float32)], *terms)


def activate(stays, came, kept, *terms):
    block = stays.shape

    def body(stays_ref, came_ref, kept_ref, *refs):
        def piece(unit, column):
            gate = stays_ref[unit, :, column] + wide(came_ref[unit, :, column])
            up = sum(wide(ref[unit, :, column]) for ref in refs[:-1]) + wide(kept_ref[0, unit, :, column])
            refs[-1][unit, :, column] = (gate / (1.0 + jnp.exp(-gate)) * up).astype(jnp.bfloat16)

        in_pieces(block, 512, piece)

    return whole_call(body, [(block, jnp.bfloat16)], stays, came, kept, *terms)[0]


def along(value, step):
    return lax.ppermute(value, "fsdp", [(i, i // RING * RING + (i + step) % RING) for i in range(2 * RING)])


def across(value):
    return lax.ppermute(value, "fsdp", [(i, (i + RING) % (2 * RING)) for i in range(2 * RING)])


def to_others(right, left, far):
    return along(right, 1), along(left, -1), along(far, 2)


def finish(full, me, info, parts, down_weight, tile):
    units, part, width = parts[0].shape
    experts, features = down_weight.shape[:2]
    rows = info.shape[0]
    count = len(parts)

    room = UNIT if units == experts else 2 * UNIT

    def body(full_ref, me_ref, info_ref, *refs):
        part_refs, (down_ref, out_ref, hidden, total) = refs[:count], refs[count:]
        local = pl.program_id(0)

        def put(slots):
            for index, ref in enumerate(part_refs):
                order, side = index // 2, index % 2
                step = (0, 1, RING - 1, 2)[order]
                target = (me_ref[0] // RING + side) % 2 * RING + (me_ref[0] + step) % RING
                for first in range(0, slots, UNIT):
                    unit = extra_unit(units, experts, local) if first else local
                    hidden[pl.ds(pl.multiple_of(target * part + first, part), part)] = ref[unit]

            def step(index, carry):
                chosen = pl.ds(pl.multiple_of(index * tile, tile), tile)
                value = dot(down_ref[local, chosen], hidden[:slots], ((1,), (1,))).astype(jnp.bfloat16)
                for expert in range(experts):

                    @pl.when(local == expert)
                    def _():
                        total[chosen, expert * room : expert * room + slots] = value

                return carry

            lax.fori_loop(0, features // tile, step, 0)

        if units < 2 * experts:

            @pl.when(full_ref[local] == 0)
            def _():
                put(UNIT)
                if units > experts:
                    for expert in range(experts):

                        @pl.when(local == expert)
                        def _():
                            total[:, expert * room + UNIT : (expert + 1) * room] = jnp.zeros((features, UNIT), jnp.bfloat16)

        if units > experts:

            @pl.when(full_ref[local] != 0)
            def _():
                put(2 * UNIT)

        @pl.when(local == experts - 1)
        def _():
            slot = lax.broadcasted_iota(jnp.int32, (rows, room), 1)
            high, low = [], []
            for expert in range(experts):
                named = info_ref[:, expert : expert + 1].astype(jnp.int32) == slot
                gate = info_ref[:, experts + expert : experts + expert + 1]
                rounded = gate.astype(jnp.bfloat16).astype(jnp.float32)
                high.append(jnp.where(named, rounded, 0.0).astype(jnp.bfloat16))
                low.append(jnp.where(named, gate - rounded, 0.0).astype(jnp.bfloat16))
            mixed = sum(dot(jnp.concatenate(side, axis=1), total[...], ((1,), (1,))) for side in (high, low))
            out_ref[...] = mixed.astype(jnp.bfloat16)

    scalars, whole = pl.BlockSpec(memory_space=pltpu.SMEM), pl.BlockSpec(memory_space=pltpu.VMEM)
    return pl.pallas_call(
        body,
        grid=(experts,),
        out_shape=jax.ShapeDtypeStruct((rows, features), jnp.bfloat16),
        in_specs=[scalars, scalars] + [whole] * (count + 2),
        out_specs=whole,
        scratch_shapes=[
            pltpu.VMEM((2 * UNIT, width), jnp.bfloat16),
            pltpu.VMEM((features, experts * room), jnp.bfloat16),
        ],
        compiler_params=params(24),
        cost_estimate=pl.CostEstimate(
            flops=2 * units * UNIT * features * width,
            bytes_accessed=2 * experts * features * width + 2 * units * UNIT * width,
            transcendentals=0,
        ),
    )(full, me, info, *parts, down_weight)


def on_device(tokens, expert_ids, combine_weight, gate_weight, up_weight, down_weight):
    exp_count, fsdp_count = lax.axis_size("exp"), lax.axis_size("fsdp")
    devices = exp_count * fsdp_count
    rows_dev, width = tokens.shape
    experts, depth, _ = gate_weight.shape
    sent = pack_rows(tokens, expert_ids, combine_weight, exp_count, fsdp_count, exp_count * experts)
    sent = sent.reshape((devices,) + sent.shape[2:])
    rows_in = lax.all_to_all(sent, BOTH, 0, 0, tiled=True).reshape(devices * rows_dev, depth + META)
    me = jnp.stack([lax.axis_index("fsdp"), lax.axis_index("exp")]).astype(jnp.int32)
    packed, info, full = gather_rows(me, rows_in, experts, exp_count * experts, 2 * UNIT)

    def routed(units, full, packed, info, gate_weight, up_weight, down_weight):
        sent, own, kept = project(full, packed, up_weight, units, True, 2048)
        packed, sent = lax.optimization_barrier((packed, sent))
        gate_kept, *gate_terms = project(full, packed, gate_weight, units, False, 2048)
        came = across(sent)
        own = across(own)
        gate_terms = to_others(*gate_terms)
        up_terms = fold(kept, came)
        gate_kept, up_terms = lax.optimization_barrier((gate_kept, up_terms))
        up_terms = to_others(*up_terms)
        sent, stays = add_along(gate_kept, *gate_terms)
        hidden = activate(stays, across(sent), kept, own, *up_terms)
        other = across(hidden)
        right, left, far = along(hidden, -1), along(hidden, 1), along(hidden, 2)
        right_other, left_other, far_other = along(other, -1), along(other, 1), across(far)
        parts = hidden, other, right, right_other, left, left_other, far, far_other
        return finish(full, me, info, parts, down_weight, 448)

    order = (experts + 1, 2 * experts, experts)
    branches = [lambda *operands, units=units: routed(units, *operands) for units in order]
    number = (jnp.sum(full) + len(order) - 1) % len(order)
    mixed = lax.switch(number, branches, full, packed, info, gate_weight, up_weight, down_weight)
    home = lax.all_to_all(mixed.reshape(devices, rows_dev, depth), BOTH, 0, 0, tiled=True)
    home = home.reshape(exp_count, fsdp_count, rows_dev, depth).astype(jnp.float32)
    return jnp.sum(home, axis=0).astype(jnp.bfloat16).transpose(1, 0, 2).reshape(rows_dev, width)


def solution(mesh):
    return jax.shard_map(
        on_device,
        mesh=mesh,
        in_specs=(
            P(BOTH, None),
            P(BOTH, None),
            P(BOTH, None),
            P("exp", "fsdp", None),
            P("exp", "fsdp", None),
            P("exp", "fsdp", None),
        ),
        out_specs=P(BOTH, None),
        check_vma=False,
    )
```
